512 devices in a mesh: grid: 128 (over x, z, core), rep: 4 (over y).
Axes of the slice: x: 4, y: 4, z: 16, core: 2. Of those that a mesh axis runs over, the one named last changes fastest.
Arguments:
- amplitudes: float32 [2048, 1440], P('grid'), may hold values from -6 to 6
- denominators: float32 [2048, 1440], P('grid'), may hold values from 0.5 to 5
- integrals: bfloat16 [737280, 1440], P(('grid', 'rep')), may hold values from -0.0390625 to 0.0390625
- amp_owner: int32 [65536, 1], P(('grid', 'rep')), may hold values from 0 to 127; in each aligned block of 128 rows (0 to 127, 128 to 255, ...) at most 2 rows name the same one
- amp_slot: int32 [65536], P(('grid', 'rep')), may hold values from 0 to 15
- res_owner: int32 [65536, 1], P(('grid', 'rep')), may hold values from 0 to 127; in each aligned block of 128 rows (0 to 127, 128 to 255, ...) at most 2 rows name the same one
- res_slot: int32 [65536], P(('grid', 'rep')), may hold values from 0 to 15
- task_count: int32 [512], P(('grid', 'rep')), may hold values from 1 to 128, 32768 in all
Outputs:
- residual: float32 [2048, 1440], P('grid')
- updated: float32 [2048, 1440], P('grid')
The draws below stay inside these ranges and needn't reach their ends.
Inputs may be any that keep to these rules, and one draw needn't show every extreme that they name: `amp_owner`: among the 128 rows of one device, at most 2 name any one owner, and in some devices one owner is named exactly 2 times. `res_owner`: among the 128 rows of one device, at most 2 name any one owner, and in some devices one owner is named exactly 2 times. `task_count`: the counts over all devices sum to 128 * 4 * 64, and some device is full.
All inputs are finite; a program needn't handle non-finite values.
Results may differ from the reference program's by a relative error of at most 0.0029.
Values may be sent and summed in bfloat16 or wider, within the bound.
No kernel may reach another device: no remote copies, remote signals or barrier semaphores. Data moves between devices by JAX's collectives and lax.ppermute only.
A program may use at most 64 MiB of HBM per device.

```python
import math
import jax
import jax.numpy as jnp
import numpy as np
from jax import lax

TILE_DEV = 16
TASKS_DEV = 128
CAP = 2
NT = 2048
OV = 1440
N_GRID = 128
N_REP = 4


def touch_ends(values, key, least, high):
    longest = values.shape.index(max(values.shape))
    spots = []
    for shift in (0, 1):
        where = [jax.random.randint(jax.random.fold_in(key, axis), (), 0, length) for axis, length in enumerate(values.shape)]
        where[longest] = (where[longest] + shift) % values.shape[longest]
        spots.append(tuple(where))
    return values.at[spots[0]].set(least).at[spots[1]].set(high)


def level_of(rng, shape, pieces, least, top_value):
    def one(dim, blocks):
        draws = jax.random.uniform(jax.random.fold_in(jax.random.fold_in(rng, 6), dim), (blocks,), jnp.float32, least / len(pieces), top_value / len(pieces))
        return jnp.repeat(jnp.exp(draws), shape[dim] // blocks).reshape((-1,) + (1,) * (len(shape) - dim - 1))

    factor_of = one(*pieces[0])
    for cut in pieces[1:]:
        factor_of = factor_of * one(*cut)
    return factor_of


def profile(count, total, most, slope):
    portions = [(1 << 20) // math.isqrt(standing ** slope) + 1 for standing in range(2, count + 1)]
    rest, given = total - most - (count - 1), [1] * (count - 1)
    while rest > 0:
        candidates = [i for i in range(count - 1) if given[i] < most]
        whole, remaining = sum([portions[i] for i in candidates]), rest
        for i in candidates:
            more = min(most - given[i], max(1, remaining * portions[i] // whole), rest)
            given[i] = given[i] + more
            rest = rest - more
    return np.array([most] + given)


def uneven_parts(stream_key, count, total, reach, lean):
    if count == 2:
        one = jax.random.randint(stream_key, (), max(1, total - reach), min(reach, total - 1) + 1)
        return jnp.stack([one, total - one])
    sizes = jnp.asarray(profile(count, total, reach, lean), jnp.int32)
    pairs = (count - 1) // 2
    donor, receiver = sizes[1:1 + 2 * pairs:2], sizes[2:2 + 2 * pairs:2]
    slack = jnp.minimum(donor - 1, reach - receiver)
    passed = jax.random.randint(jax.random.fold_in(stream_key, 1), (pairs,), 0, 1 << 20) % (slack + 1)
    sizes = sizes.at[1:1 + 2 * pairs:2].set(donor - passed).at[2:2 + 2 * pairs:2].set(receiver + passed)
    return sizes[jax.random.permutation(jax.random.fold_in(stream_key, 2), count)]


def assign_block(key, own, number, rows, amount, top, bound, skew):
    ranking = jax.random.permutation(key, amount)
    crowded, ordinary = shares(amount, rows * top, bound, skew, True), shares(amount, rows * top, bound, skew, False)
    places = jnp.arange(amount)

    def named(sizes, turn):
        used = int((sizes > 0).sum())
        fixed = max(1, used // 4)
        moved = fixed + (places - fixed + turn * (used - fixed)) % max(1, amount - fixed)
        return jnp.zeros((amount,), jnp.int32).at[ranking[jnp.where(places < fixed, places, moved)]].set(jnp.asarray(sizes, jnp.int32))

    sizes = jnp.where(number % 4 == 0, named(crowded, number // 4), named(ordinary, number - number // 4 - 1))
    mixed = jax.random.permutation(jax.random.fold_in(own, 3), amount)
    source_of, taker = mixed[0:amount // 2 * 2:2], mixed[1:amount // 2 * 2:2]
    margin = jnp.minimum(sizes[source_of] - 1, bound - sizes[taker]) // 2
    margin = jnp.where((source_of == ranking[0]) | (taker == ranking[0]) | (sizes[taker] == 0), 0, jnp.maximum(margin, 0))
    moved = jax.random.randint(jax.random.fold_in(own, 4), (amount // 2,), 0, 1 << 20) % (margin + 1)
    sizes = sizes.at[source_of].add(-moved).at[taker].add(moved)
    members = jnp.searchsorted(jnp.cumsum(sizes), jnp.arange(rows * top), side="right").astype(jnp.int32)
    table = members.reshape(top, rows).T
    table = table[jax.random.permutation(jax.random.fold_in(own, 1), rows)]
    turn = jax.random.randint(jax.random.fold_in(own, 2), (rows, 1), 0, top)
    return jnp.take_along_axis(table, (jnp.arange(top)[None, :] + turn) % top, axis=1)


def shares(count, total, limit, lean, full):
    weights = [(1 << 20) // math.isqrt(standing ** lean) + 1 for standing in range(1, count + 1)]
    largest = limit if full else min(limit, max(-(-total // count), total * weights[0] // sum(weights)))
    least = 1 if total - largest >= count - 1 else 0
    given, surplus = [largest] + [least] * (count - 1), total - largest - least * (count - 1)
    while surplus > 0:
        free = [i for i in range(1, count) if given[i] < largest] or [i for i in range(1, count) if given[i] < limit]
        mass, remaining = sum([weights[i] for i in free]), surplus
        for i in free:
            more = min(limit - given[i], max(1, remaining * weights[i] // mass), surplus)
            given[i] = given[i] + more
            surplus = surplus - more
    return np.array(given)


def scatter_about(rng, dims, deviation, limit, cuts=(), held_as=jnp.bfloat16):
    level = level_of(rng, dims, cuts, -0.22, 0.18) if cuts else 1.0
    drawn = jax.random.normal(rng, dims, jnp.float32) * deviation * level
    return jnp.minimum(jnp.maximum(drawn, -limit), limit).astype(held_as)


def setup_inputs(seed: int = 0) -> dict:
    key_of = jax.random.split(jax.random.key(seed), 9)
    amplitudes = scatter_about(key_of[0], (NT, OV), 1.0, 6.0, ((0, 128),), jnp.float32)
    denominators = jnp.clip(jnp.exp(math.log(5.0) - 2.3025851 * jax.random.uniform(key_of[1], (NT, OV), jnp.float32) ** level_of(key_of[1], (NT, OV), ((0, 128),), -0.2, 0.2)), 0.5, 5.0)
    integrals = scatter_about(key_of[2], (N_GRID * N_REP * OV, OV), (OV * N_REP * TASKS_DEV // (2 * TILE_DEV)) ** -0.5, 0.0390625, ((0, 512),))
    amp_owner_keys = jax.random.split(jax.random.fold_in(key_of[3], 1), (N_GRID * N_REP * TASKS_DEV) // TASKS_DEV)
    amp_owner_turns = jax.random.permutation(jax.random.fold_in(key_of[3], 3), (N_GRID * N_REP * TASKS_DEV) // TASKS_DEV)
    amp_owner = jax.vmap(lambda own, number: assign_block(jax.random.fold_in(key_of[3], 2), own, number, TASKS_DEV, N_GRID, 1, CAP, 2))(amp_owner_keys, amp_owner_turns).reshape((N_GRID * N_REP * TASKS_DEV, 1))
    amp_slot = touch_ends(jax.random.randint(key_of[4], (N_GRID * N_REP * TASKS_DEV,), 0, TILE_DEV), jax.random.fold_in(key_of[4], 1), 0, TILE_DEV - 1).astype(jnp.int32)
    res_owner_keys = jax.random.split(jax.random.fold_in(key_of[5], 1), (N_GRID * N_REP * TASKS_DEV) // TASKS_DEV)
    res_owner_turns = jax.random.permutation(jax.random.fold_in(key_of[5], 3), (N_GRID * N_REP * TASKS_DEV) // TASKS_DEV)
    res_owner = jax.vmap(lambda own, number: assign_block(jax.random.fold_in(key_of[5], 2), own, number, TASKS_DEV, N_GRID, 1, CAP, 1))(res_owner_keys, res_owner_turns).reshape((N_GRID * N_REP * TASKS_DEV, 1))
    res_slot = touch_ends(jax.random.randint(key_of[6], (N_GRID * N_REP * TASKS_DEV,), 0, TILE_DEV), jax.random.fold_in(key_of[6], 1), 0, TILE_DEV - 1).astype(jnp.int32)
    task_count = uneven_parts(key_of[7], N_GRID * N_REP, N_GRID * N_REP * TASKS_DEV // 2, TASKS_DEV, 2).astype(jnp.int32)
    return {"amplitudes": amplitudes, "denominators": denominators, "integrals": integrals, "amp_owner": amp_owner, "amp_slot": amp_slot, "res_owner": res_owner, "res_slot": res_slot, "task_count": task_count}


def reference(amplitudes, denominators, integrals, amp_owner, amp_slot, res_owner, res_slot, task_count):
    tile_total = amplitudes.shape[0]

    def one_device(summed, device):
        first_row = device * TASKS_DEV
        owners = lax.dynamic_slice_in_dim(amp_owner[:, 0], first_row, TASKS_DEV)
        slots = lax.dynamic_slice_in_dim(amp_slot, first_row, TASKS_DEV)
        targets_owner = lax.dynamic_slice_in_dim(res_owner[:, 0], first_row, TASKS_DEV)
        targets_slot = lax.dynamic_slice_in_dim(res_slot, first_row, TASKS_DEV)
        source = (owners * TILE_DEV + slots).astype(jnp.int32)
        operand = amplitudes[source].astype(jnp.bfloat16)
        block = lax.dynamic_slice_in_dim(integrals, (device * OV).astype(jnp.int32), OV)
        contrib = jnp.dot(operand, block, preferred_element_type=jnp.float32)
        active = jnp.arange(TASKS_DEV, dtype=jnp.int32) < task_count[device]
        contrib = jnp.where(active[:, None], contrib, jnp.zeros_like(contrib))
        target = (targets_owner * TILE_DEV + targets_slot).astype(jnp.int32)
        summed = summed + jax.ops.segment_sum(contrib, target, num_segments=tile_total)
        return summed, None

    start = jnp.zeros(amplitudes.shape, jnp.float32)
    devices = jnp.arange(N_GRID * N_REP, dtype=jnp.int32)
    residual, unused = lax.scan(one_device, start, devices)
    updated = amplitudes + residual / denominators
    return residual, updated
```

```python
import jax
import jax.numpy as jnp
from jax import lax
from jax.experimental import pallas as pl
from jax.experimental.pallas import tpu as pltpu
from jax.sharding import Mesh, PartitionSpec as P

BF = jnp.bfloat16
F32 = jnp.float32
I32 = jnp.int32
TASKS = 128
PEERS = 64
CELLS = 256
WIDTH = 1440
BLOCK = ("x", "zl", "core", "rep")
RING = ("zh", "rep")


def iota(shape, dim):
    return lax.broadcasted_iota(I32, shape, dim)


def dot(a, b):
    return lax.dot_general(a, b, (((1,), (0,)), ((), ())), preferred_element_type=F32)


def cells(owner, rank):
    core = owner & 1
    zl = (owner >> 1) & 1
    zh = (owner >> 2) & 7
    x = owner >> 5
    peer = ((x * 2 + zl) * 2 + core) * 4 + (zh & 3)
    return peer * 4 + (zh >> 2) * 2 + rank


def place(owner_col):
    square = (TASKS, TASKS)
    row, col = iota(square, 0), iota(square, 1)
    owner_row = jnp.sum(jnp.where(row == col, owner_col, 0), axis=0, keepdims=True)
    same = owner_col == owner_row
    rank_col = jnp.sum(jnp.where(same & (col < row), 1, 0), axis=1, keepdims=True)
    rank_row = jnp.sum(jnp.where(same & (row < col), 1, 0), axis=0, keepdims=True)
    return cells(owner_col, rank_col), cells(owner_row, rank_row)


def to_col(row_vec):
    square = (TASKS, TASKS)
    return jnp.sum(jnp.where(iota(square, 0) == iota(square, 1), row_vec, 0), axis=1, keepdims=True)


def index_kernel(count_ref, ao_ref, as_ref, ro_ref, rs_ref, want_ref, gather_ref, scatter_ref):
    count = count_ref[0]
    live_col = iota((TASKS, 1), 0) < count
    live_row = iota((1, TASKS), 1) < count
    total = jnp.zeros((PEERS, 8), F32)
    for which, (o_ref, s_ref) in enumerate(((ao_ref, as_ref), (ro_ref, rs_ref))):
        col, row = place(o_ref[...])
        slot = to_col(s_ref[...])
        lane = iota((TASKS, 8), 1)
        value = jnp.where((lane == (col & 3) + 4 * which) & live_col, slot + 1, 0)
        peer = jnp.where(iota((PEERS, TASKS), 0) == (row >> 2), 1.0, 0.0)
        total = total + dot(peer.astype(BF), value.astype(F32).astype(BF))
        if which == 0:
            hit = (iota((TASKS, CELLS), 1) == col) & live_col
            gather_ref[...] = jnp.where(hit, 1.0, 0.0).astype(BF)
        else:
            hit = (iota((CELLS, TASKS), 0) == row) & live_row
            scatter_ref[...] = jnp.where(hit, 1.0, 0.0).astype(BF)
    want_ref[...] = total.astype(I32) - 1


def picks(want, half, first):
    spread = jnp.where(iota((CELLS, PEERS), 0) >> 2 == iota((CELLS, PEERS), 1), 1.0, 0.0)
    every = dot(spread.astype(BF), want.astype(F32).astype(BF)).astype(I32)
    cell = iota((CELLS, 8), 0)
    mine = iota((CELLS, 8), 1) == (cell & 3) + first
    slot = jnp.sum(jnp.where(mine, every, 0), axis=1, keepdims=True)
    part = (iota((CELLS, 1), 0) >> 1) & 1
    held = jnp.where(slot < 0, -1, jnp.bitwise_xor(part, half) * 16 + slot)
    return jnp.where(iota((CELLS, 32), 1) == held, 1.0, 0.0).astype(BF)


def answer_kernel(half_ref, want_ref, near_ref, far_ref, out_ref):
    rows = jnp.concatenate([near_ref[...], far_ref[...]], axis=0)
    out_ref[...] = dot(picks(want_ref[...], half_ref[0], 0), rows).astype(BF)


def task_kernel(gather_ref, rows_ref, scatter_ref, tile_ref, out_ref):
    operand = dot(gather_ref[...], rows_ref[...]).astype(BF)
    contrib = dot(operand, tile_ref[...]).astype(BF)
    out_ref[...] = dot(scatter_ref[...], contrib).astype(BF)


def collect_kernel(half_ref, want_ref, rows_ref, near_ref, far_ref):
    onehot = picks(want_ref[...], half_ref[0], 4)
    part = lax.dot_general(
        onehot, rows_ref[...], (((0,), (0,)), ((), ())), preferred_element_type=F32
    )
    near_ref[...] = part[:16].astype(BF)
    far_ref[...] = part[16:].astype(BF)


VM = pl.BlockSpec(memory_space=pltpu.VMEM)
SM = pl.BlockSpec(memory_space=pltpu.SMEM)


def call(kernel, ins, outs, *args, limit=16 << 20):
    shapes = tuple(jax.ShapeDtypeStruct(s, d) for s, d in outs)
    return pl.pallas_call(
        kernel,
        out_shape=shapes,
        in_specs=list(ins),
        out_specs=tuple(VM for _ in shapes),
        compiler_params=pltpu.CompilerParams(vmem_limit_bytes=limit),
    )(*args)


def spread_pairs(turn):
    pairs = []
    for zh in range(8):
        for y in range(4):
            pairs.append(((4 * ((zh // 4) ^ turn) + y) * 4 + zh % 4, zh * 4 + y))
    return pairs


def per_device(
    amplitudes, denominators, integrals, amp_owner, amp_slot, res_owner, res_slot, task_count
):
    half = (lax.axis_index("zh") // 4).astype(I32).reshape(1)
    low = amplitudes.astype(BF)
    near = lax.ppermute(low, RING, spread_pairs(0))
    far = lax.ppermute(low, RING, spread_pairs(1))
    want, gather, scatter = call(
        index_kernel,
        (SM, VM, VM, VM, VM),
        (((PEERS, 8), I32), ((TASKS, CELLS), BF), ((CELLS, TASKS), BF)),
        task_count,
        amp_owner,
        amp_slot.reshape(1, TASKS),
        res_owner,
        res_slot.reshape(1, TASKS),
    )
    wanted = lax.all_to_all(want.reshape(PEERS, 1, 8), BLOCK, 0, 0, tiled=True).reshape(PEERS, 8)
    (found,) = call(
        answer_kernel, (SM, VM, VM, VM), (((CELLS, WIDTH), BF),), half, wanted, near, far
    )
    fetched = lax.all_to_all(found.reshape(PEERS, 4, WIDTH), BLOCK, 0, 0, tiled=True)
    (sent,) = call(
        task_kernel,
        (VM, VM, VM, VM),
        (((CELLS, WIDTH), BF),),
        gather,
        fetched.reshape(CELLS, WIDTH),
        scatter,
        integrals,
        limit=32 << 20,
    )
    landed = lax.all_to_all(sent.reshape(PEERS, 4, WIDTH), BLOCK, 0, 0, tiled=True)
    part0, part1 = call(
        collect_kernel,
        (SM, VM, VM),
        (((16, WIDTH), BF), ((16, WIDTH), BF)),
        half,
        wanted,
        landed.reshape(CELLS, WIDTH),
    )
    back0 = lax.ppermute(part0, RING, [(d, s) for s, d in spread_pairs(0)])
    back1 = lax.ppermute(part1, RING, [(d, s) for s, d in spread_pairs(1)])
    mine = back0.astype(F32) + back1.astype(F32)
    copies = jnp.broadcast_to(mine[None], (4, 16, WIDTH))
    every = lax.all_to_all(copies, "rep", 0, 0, tiled=True)
    residual = jnp.sum(every, axis=0)
    return residual, amplitudes + residual / denominators


def solution(mesh):
    fine = Mesh(mesh.devices.reshape(4, 8, 2, 2, 4), ("x", "zh", "zl", "core", "rep"))
    grid = ("x", "zh", "zl", "core")
    every = grid + ("rep",)
    return jax.shard_map(
        per_device,
        mesh=fine,
        in_specs=(
            P(grid, None),
            P(grid, None),
            P(every, None),
            P(every, None),
            P(every),
            P(every, None),
            P(every),
            P(every),
        ),
        out_specs=(P(grid, None), P(grid, None)),
        check_vma=False,
    )
```

```python
import jax
import jax.numpy as jnp
from jax import lax
from jax.experimental import pallas as pl
from jax.experimental.pallas import tpu as pltpu
from jax.sharding import Mesh, PartitionSpec as P

BF = jnp.bfloat16
F32 = jnp.float32
I32 = jnp.int32
TASKS = 128
PEERS = 64
CELLS = 256
WIDTH = 1440
SWAPS = (True, True)
CHUNKS = ((0, 384), (384, 384), (768, 384), (1152, 288))
BLOCK = ("x", "zl", "core", "rep")
RING = ("zh", "rep")


def iota(shape, dim):
    return lax.broadcasted_iota(I32, shape, dim)


def dot(a, b):
    return lax.dot_general(a, b, (((1,), (0,)), ((), ())), preferred_element_type=F32)


def cells(owner, rank, swap):
    core = owner & 1
    zl = (owner >> 1) & 1
    zh = (owner >> 2) & 7
    x = owner >> 5
    first, second = (zh >> 2, core) if swap else (core, zh >> 2)
    peer = ((x * 2 + zl) * 2 + first) * 4 + (zh & 3)
    return peer * 4 + second * 2 + rank


def place(owner_col, owner_row, swap):
    square = (TASKS, TASKS)
    row, col = iota(square, 0), iota(square, 1)
    same = owner_col == owner_row
    rank_col = jnp.sum(jnp.where(same & (col < row), 1, 0), axis=1, keepdims=True)
    rank_row = jnp.sum(jnp.where(same & (row < col), 1, 0), axis=0, keepdims=True)
    return cells(owner_col, rank_col, swap), cells(owner_row, rank_row, swap)


def to_col(row_vec):
    square = (TASKS, TASKS)
    return jnp.sum(jnp.where(iota(square, 0) == iota(square, 1), row_vec, 0), axis=1, keepdims=True)


def index_kernel(
    count_ref, ao_hbm, as_hbm, ro_hbm, rs_hbm, want_ref, gather_ref, scatter_ref,
    ao_ref, as_ref, ro_ref, rs_ref, sems,
):
    moves = [
        pltpu.make_async_copy(src, dst, sems.at[i])
        for i, (src, dst) in enumerate(
            ((ao_hbm, ao_ref), (as_hbm, as_ref), (ro_hbm, ro_ref), (rs_hbm, rs_ref))
        )
    ]
    for move in moves:
        move.start()
    for move in moves:
        move.wait()
    count = count_ref[0]
    live_col = iota((TASKS, 1), 0) < count
    live_row = iota((1, TASKS), 1) < count
    total = jnp.zeros((PEERS, 8), F32)
    for which, (o_ref, s_ref) in enumerate(((ao_ref, as_ref), (ro_ref, rs_ref))):
        owner = o_ref[...]
        col, row = place(to_col(owner), owner, SWAPS[which])
        slot = to_col(s_ref[...])
        lane = iota((TASKS, 8), 1)
        value = jnp.where((lane == (col & 3) + 4 * which) & live_col, slot + 1, 0)
        peer = jnp.where(iota((PEERS, TASKS), 0) == (row >> 2), 1.0, 0.0)
        total = total + dot(peer.astype(BF), value.astype(F32).astype(BF))
        if which == 0:
            hit = (iota((TASKS, CELLS), 1) == col) & live_col
            gather_ref[...] = jnp.where(hit, 1.0, 0.0).astype(BF)
        else:
            hit = (iota((CELLS, TASKS), 0) == row) & live_row
            scatter_ref[...] = jnp.where(hit, 1.0, 0.0).astype(BF)
    want_ref[...] = total.astype(I32) - 1


def picks(want, half, first):
    spread = jnp.where(iota((CELLS, PEERS), 0) >> 2 == iota((CELLS, PEERS), 1), 1.0, 0.0)
    every = dot(spread.astype(BF), want.astype(F32).astype(BF)).astype(I32)
    cell = iota((CELLS, 8), 0)
    mine = iota((CELLS, 8), 1) == (cell & 3) + first
    slot = jnp.sum(jnp.where(mine, every, 0), axis=1, keepdims=True)
    part = (iota((CELLS, 1), 0) >> 1) & 1
    held = jnp.where(slot < 0, -1, jnp.bitwise_xor(part, half) * 16 + slot)
    return jnp.where(iota((CELLS, 32), 1) == held, 1.0, 0.0).astype(BF)


def answer_kernel(half_ref, want_ref, rows_ref, out_ref):
    out_ref[...] = dot(picks(want_ref[...], half_ref[0], 0), rows_ref[...]).astype(BF)


def task_kernel(gather_ref, rows_ref, scatter_ref, tile_hbm, out_ref, tile_ref, sems):
    loads = [
        pltpu.make_async_copy(tile_hbm.at[pl.ds(k, n)], tile_ref.at[pl.ds(k, n)], sems.at[i])
        for i, (k, n) in enumerate(CHUNKS)
    ]
    for load in loads:
        load.start()
    operand = dot(gather_ref[...], rows_ref[...]).astype(BF)
    total = jnp.zeros((TASKS, WIDTH), F32)
    for load, (k, n) in zip(loads, CHUNKS):
        load.wait()
        total = total + dot(operand[:, k : k + n], tile_ref[k : k + n, :])
    out_ref[...] = dot(scatter_ref[...], total.astype(BF)).astype(BF)


def collect_kernel(want_ref, rows_ref, out_ref):
    onehot = picks(want_ref[...], 0, 4)
    part = lax.dot_general(
        onehot, rows_ref[...], (((0,), (0,)), ((), ())), preferred_element_type=F32
    )
    out_ref[...] = part.astype(BF)


VM = pl.BlockSpec(memory_space=pltpu.VMEM)
SM = pl.BlockSpec(memory_space=pltpu.SMEM)
HB = pl.BlockSpec(memory_space=pl.ANY)


def call(kernel, ins, outs, *args, scratch=(), limit=None):
    shapes = tuple(jax.ShapeDtypeStruct(s, d) for s, d in outs)
    return pl.pallas_call(
        kernel,
        out_shape=shapes,
        in_specs=list(ins),
        out_specs=tuple(VM for _ in shapes),
        scratch_shapes=list(scratch),
        compiler_params=pltpu.CompilerParams(vmem_limit_bytes=limit),
    )(*args)


def spread_pairs(turn):
    pairs = []
    for zh in range(8):
        for y in range(4):
            pairs.append(((4 * ((zh // 4) ^ turn) + y) * 4 + zh % 4, zh * 4 + y))
    return pairs


def return_pairs():
    pairs = []
    for a in range(2):
        for b in range(4):
            for k in range(2):
                for y in range(4):
                    pairs.append((((4 * a + b) * 2 + k) * 4 + y, ((4 * k + y) * 2 + a) * 4 + b))
    return pairs


def per_device(
    amplitudes, denominators, integrals, amp_owner, amp_slot, res_owner, res_slot, task_count
):
    half = (lax.axis_index("zh") // 4).astype(I32).reshape(1)
    other = lax.optimization_barrier(lax.ppermute(amplitudes, "core", ((0, 1), (1, 0))))
    pair = jnp.concatenate([amplitudes.astype(BF), other.astype(BF)])
    want, gather, scatter = call(
        index_kernel,
        (SM, HB, HB, HB, HB),
        (((PEERS, 8), I32), ((TASKS, CELLS), BF), ((CELLS, TASKS), BF)),
        task_count,
        amp_owner.reshape(1, TASKS),
        amp_slot.reshape(1, TASKS),
        res_owner.reshape(1, TASKS),
        res_slot.reshape(1, TASKS),
        scratch=[pltpu.VMEM((1, TASKS), I32)] * 4 + [pltpu.SemaphoreType.DMA((4,))],
    )
    pair, want = lax.optimization_barrier((pair, want))
    held = lax.ppermute(pair, ("zh", "core", "rep"), [(d, s) for s, d in return_pairs()])
    wanted = lax.all_to_all(want.reshape(PEERS, 1, 8), BLOCK, 0, 0, tiled=True).reshape(PEERS, 8)
    (found,) = call(
        answer_kernel, (SM, VM, VM), (((CELLS, WIDTH), BF),), half, wanted, held,
        limit=16 << 20,
    )
    fetched = lax.all_to_all(found.reshape(PEERS, 4, WIDTH), BLOCK, 0, 0, tiled=True)
    (sent,) = call(
        task_kernel,
        (VM, VM, VM, HB),
        (((CELLS, WIDTH), BF),),
        gather,
        fetched.reshape(CELLS, WIDTH),
        scatter,
        integrals,
        scratch=[pltpu.VMEM((WIDTH, WIDTH), BF), pltpu.SemaphoreType.DMA((len(CHUNKS),))],
        limit=50 << 20,
    )
    landed = lax.all_to_all(sent.reshape(PEERS, 4, WIDTH), BLOCK, 0, 0, tiled=True)
    (part,) = call(
        collect_kernel,
        (VM, VM),
        (((32, WIDTH), BF),),
        wanted,
        landed.reshape(CELLS, WIDTH),
        limit=16 << 20,
    )
    back = lax.ppermute(part, ("zh", "core", "rep"), return_pairs())
    copies = jnp.broadcast_to(back.reshape(2, 1, 16, WIDTH), (2, 4, 16, WIDTH))
    every = lax.all_to_all(copies.reshape(8, 16, WIDTH), ("core", "rep"), 0, 0, tiled=True)
    residual = jnp.sum(every.astype(F32), axis=0)
    return residual, amplitudes + residual / denominators


def solution(mesh):
    fine = Mesh(mesh.devices.reshape(4, 8, 2, 2, 4), ("x", "zh", "zl", "core", "rep"))
    grid = ("x", "zh", "zl", "core")
    every = grid + ("rep",)
    return jax.shard_map(
        per_device,
        mesh=fine,
        in_specs=(
            P(grid, None),
            P(grid, None),
            P(every, None),
            P(every, None),
            P(every),
            P(every, None),
            P(every),
            P(every),
        ),
        out_specs=(P(grid, None), P(grid, None)),
        check_vma=False,
    )
```

```python
import jax
import jax.numpy as jnp
from jax import lax
from jax.experimental import pallas as pl
from jax.experimental.pallas import tpu as pltpu
from jax.sharding import Mesh, PartitionSpec as P

BF = jnp.bfloat16
F32 = jnp.float32
I32 = jnp.int32
TASKS = 128
PEERS = 64
CELLS = 256
WIDTH = 1440
CHUNKS = ((0, 384), (384, 384), (768, 384), (1152, 288))
BLOCK = ("core", "x", "zl", "rep")
RING = ("zh", "core", "rep")


def iota(shape, dim):
    return lax.broadcasted_iota(I32, shape, dim)


def dot(a, b, side=1):
    return lax.dot_general(a, b, (((side,), (0,)), ((), ())), preferred_element_type=F32)


def cells(owner, rank):
    core = owner & 1
    zl = (owner >> 1) & 1
    zh = (owner >> 2) & 7
    x = owner >> 5
    peer = (((zh >> 2) * 4 + x) * 2 + zl) * 4 + (zh & 3)
    return peer * 4 + core * 2 + rank


def index_kernel(
    count_ref, ao_hbm, as_hbm, ro_hbm, rs_hbm, want_ref, place_ref,
    ao_ref, as_ref, ro_ref, rs_ref, sems,
):
    moves = [
        pltpu.make_async_copy(src, dst, sems.at[i])
        for i, (src, dst) in enumerate(
            ((ao_hbm, ao_ref), (as_hbm, as_ref), (ro_hbm, ro_ref), (rs_hbm, rs_ref))
        )
    ]
    for move in moves:
        move.start()
    for move in moves:
        move.wait()
    square = (TASKS, TASKS)
    row, col = iota(square, 0), iota(square, 1)

    def to_col(vec):
        return jnp.sum(jnp.where(row == col, vec, 0), axis=1, keepdims=True)

    live_col = iota((TASKS, 1), 0) < count_ref[0]
    live_row = iota((1, TASKS), 1) < count_ref[0]
    total = jnp.zeros((PEERS, 8), F32)
    places = []
    for which, (o_ref, s_ref) in enumerate(((ao_ref, as_ref), (ro_ref, rs_ref))):
        owner_row = o_ref[...]
        owner_col = to_col(owner_row)
        same = owner_col == owner_row
        rank_col = jnp.sum(jnp.where(same & (col < row), 1, 0), axis=1, keepdims=True)
        rank_row = jnp.sum(jnp.where(same & (row < col), 1, 0), axis=0, keepdims=True)
        place_col = cells(owner_col, rank_col)
        place_row = cells(owner_row, rank_row)
        lane = iota((TASKS, 8), 1)
        mine = (lane == (place_col & 3) + 4 * which) & live_col
        value = jnp.where(mine, to_col(s_ref[...]) + 1, 0)
        peer = jnp.where(iota((PEERS, TASKS), 0) == (place_row >> 2), 1.0, 0.0)
        total = total + dot(peer.astype(BF), value.astype(F32).astype(BF))
        places.append(jnp.where(live_row, place_row, -1))
    want_ref[...] = total.astype(I32) - 1
    which = iota((8, TASKS), 0)
    place_ref[...] = jnp.where(which == 0, places[0], places[1])


def picks(want, swap, first):
    spread = jnp.where(iota((CELLS, PEERS), 0) >> 2 == iota((CELLS, PEERS), 1), 1.0, 0.0)
    every = dot(spread.astype(BF), want.astype(F32).astype(BF)).astype(I32)
    cell = iota((CELLS, 8), 0)
    mine = iota((CELLS, 8), 1) == (cell & 3) + first
    slot = jnp.sum(jnp.where(mine, every, 0), axis=1, keepdims=True)
    part = (iota((CELLS, 1), 0) >> 1) & 1
    held = jnp.where(slot < 0, -1, jnp.bitwise_xor(part, swap) * 16 + slot)
    return jnp.where(iota((CELLS, 32), 1) == held, 1.0, 0.0).astype(BF)


def answer_kernel(half_ref, want_ref, rows_ref, out_ref):
    out_ref[...] = dot(picks(want_ref[...], half_ref[0], 0), rows_ref[...]).astype(BF).reshape(PEERS, 4, WIDTH)


def task_kernel(place_ref, rows_ref, tile_hbm, out_ref, tile_ref, sems):
    loads = [
        pltpu.make_async_copy(tile_hbm.at[pl.ds(k, n)], tile_ref.at[pl.ds(k, n)], sems.at[i])
        for i, (k, n) in enumerate(CHUNKS)
    ]
    for load in loads:
        load.start()
    cell = iota((CELLS, TASKS), 0)
    gather = jnp.where(cell == place_ref[0:1, :], 1.0, 0.0).astype(BF)
    scatter = jnp.where(cell == place_ref[1:2, :], 1.0, 0.0).astype(BF)
    operand = dot(gather, rows_ref[...], 0).astype(BF)
    total = jnp.zeros((TASKS, WIDTH), F32)
    for load, (k, n) in zip(loads, CHUNKS):
        load.wait()
        total = total + dot(operand[:, k : k + n], tile_ref[k : k + n, :])
    out_ref[...] = dot(scatter, total.astype(BF)).astype(BF).reshape(PEERS, 4, WIDTH)


def collect_kernel(want_ref, rows_ref, out_ref):
    out_ref[...] = dot(picks(want_ref[...], 0, 4), rows_ref[...].reshape(CELLS, WIDTH), 0).astype(BF)


VM = pl.BlockSpec(memory_space=pltpu.VMEM)
SM = pl.BlockSpec(memory_space=pltpu.SMEM)
HB = pl.BlockSpec(memory_space=pl.ANY)


def call(kernel, ins, outs, *args, scratch=(), limit=None):
    shapes = tuple(jax.ShapeDtypeStruct(s, d) for s, d in outs)
    return pl.pallas_call(
        kernel,
        out_shape=shapes,
        in_specs=list(ins),
        out_specs=tuple(VM for _ in shapes),
        scratch_shapes=list(scratch),
        compiler_params=pltpu.CompilerParams(vmem_limit_bytes=limit),
    )(*args)


def return_pairs():
    pairs = []
    for a in range(2):
        for b in range(4):
            for k in range(2):
                for y in range(4):
                    pairs.append((((4 * a + b) * 2 + k) * 4 + y, ((4 * k + y) * 2 + a) * 4 + b))
    return pairs


def per_device(
    amplitudes, denominators, integrals, amp_owner, amp_slot, res_owner, res_slot, task_count
):
    half = (lax.axis_index("zh") // 4).astype(I32).reshape(1)
    other = lax.optimization_barrier(lax.ppermute(amplitudes, "core", ((0, 1), (1, 0))))
    pair = jnp.concatenate([amplitudes, other]).astype(BF)
    want, place = call(
        index_kernel,
        (SM, HB, HB, HB, HB),
        (((PEERS, 8), I32), ((8, TASKS), I32)),
        task_count,
        amp_owner.reshape(1, TASKS),
        amp_slot.reshape(1, TASKS),
        res_owner.reshape(1, TASKS),
        res_slot.reshape(1, TASKS),
        scratch=[pltpu.VMEM((1, TASKS), I32)] * 4 + [pltpu.SemaphoreType.DMA((4,))],
    )
    pair, want = lax.optimization_barrier((pair, want))
    held = lax.ppermute(pair, RING, [(d, s) for s, d in return_pairs()])
    wanted = lax.all_to_all(want.reshape(PEERS, 1, 8), BLOCK, 0, 0, tiled=True).reshape(PEERS, 8)
    (found,) = call(
        answer_kernel,
        (SM, VM, VM),
        (((PEERS, 4, WIDTH), BF),),
        half,
        wanted,
        held,
        limit=16 << 20,
    )
    fetched = lax.all_to_all(found, BLOCK, 0, 0, tiled=True)
    (sent,) = call(
        task_kernel,
        (VM, VM, HB),
        (((PEERS, 4, WIDTH), BF),),
        place,
        fetched.reshape(CELLS, WIDTH),
        integrals,
        scratch=[pltpu.VMEM((WIDTH, WIDTH), BF), pltpu.SemaphoreType.DMA((len(CHUNKS),))],
        limit=50 << 20,
    )
    landed = lax.all_to_all(sent, BLOCK, 0, 0, tiled=True)
    (part,) = call(
        collect_kernel,
        (VM, VM),
        (((32, WIDTH), BF),),
        wanted,
        landed,
        limit=16 << 20,
    )
    back = lax.ppermute(part, RING, return_pairs())
    copies = jnp.broadcast_to(back.reshape(2, 1, 16, WIDTH), (2, 4, 16, WIDTH))
    every = lax.all_to_all(copies.reshape(8, 16, WIDTH), ("core", "rep"), 0, 0, tiled=True)
    residual = jnp.sum(every.astype(F32), axis=0)
    return residual, amplitudes + residual / denominators


def solution(mesh):
    fine = Mesh(mesh.devices.reshape(4, 8, 2, 2, 4), ("x", "zh", "zl", "core", "rep"))
    grid = ("x", "zh", "zl", "core")
    every = grid + ("rep",)
    return jax.shard_map(
        per_device,
        mesh=fine,
        in_specs=(
            P(grid, None),
            P(grid, None),
            P(every, None),
            P(every, None),
            P(every),
            P(every, None),
            P(every),
            P(every),
        ),
        out_specs=(P(grid, None), P(grid, None)),
        check_vma=False,
    )
```

```python
import jax
import jax.numpy as jnp
from jax import lax
from jax.experimental import pallas as pl
from jax.experimental.pallas import tpu as pltpu
from jax.sharding import Mesh, PartitionSpec as P

BF = jnp.bfloat16
F32 = jnp.float32
I32 = jnp.int32
TASKS = 128
PEERS = 64
CELLS = 256
WIDTH = 1440
CHUNKS = ((0, 384), (384, 384), (768, 384), (1152, 288))
BLOCK = ("core", "x", "zl", "rep")
RING = ("zh", "core", "rep")


def iota(shape, dim):
    return lax.broadcasted_iota(I32, shape, dim)


def dot(a, b, side=1):
    return lax.dot_general(a, b, (((side,), (0,)), ((), ())), preferred_element_type=F32)


def cells(owner, rank):
    core = owner & 1
    zl = (owner >> 1) & 1
    zh = (owner >> 2) & 7
    x = owner >> 5
    peer = (((zh >> 2) * 4 + x) * 2 + zl) * 4 + (zh & 3)
    return peer * 4 + core * 2 + rank


def index_kernel(
    count_ref, ao_hbm, as_hbm, ro_hbm, rs_hbm, want_ref, place_ref,
    ao_ref, as_ref, ro_ref, rs_ref, sems,
):
    moves = [
        pltpu.make_async_copy(src, dst, sems.at[i])
        for i, (src, dst) in enumerate(
            ((ao_hbm, ao_ref), (as_hbm, as_ref), (ro_hbm, ro_ref), (rs_hbm, rs_ref))
        )
    ]
    for move in moves:
        move.start()
    for move in moves:
        move.wait()
    square = (TASKS, TASKS)
    row, col = iota(square, 0), iota(square, 1)

    def to_col(vec):
        return jnp.sum(jnp.where(row == col, vec, 0), axis=1, keepdims=True)

    live_row = iota((1, TASKS), 1) < count_ref[0]
    total = jnp.zeros((PEERS, 8), F32)
    places = []
    for which, (o_ref, s_ref) in enumerate(((ao_ref, as_ref), (ro_ref, rs_ref))):
        owner_row = o_ref[...]
        same = to_col(owner_row) == owner_row
        rank = jnp.sum(jnp.where(same & (row < col), 1, 0), axis=0, keepdims=True)
        place = cells(owner_row, rank)
        mine = (iota((8, TASKS), 0) == (place & 3) + 4 * which) & live_row
        value = jnp.where(mine, s_ref[...] + 1, 0)
        peer = jnp.where(iota((PEERS, TASKS), 0) == (place >> 2), 1.0, 0.0)
        total = total + lax.dot_general(
            peer.astype(BF),
            value.astype(F32).astype(BF),
            (((1,), (1,)), ((), ())),
            preferred_element_type=F32,
        )
        places.append(jnp.where(live_row, place, -1))
    want_ref[...] = total.astype(I32) - 1
    which = iota((8, TASKS), 0)
    place_ref[...] = jnp.where(which == 0, places[0], places[1])


def picks(want, swap, first):
    spread = jnp.where(iota((CELLS, PEERS), 0) >> 2 == iota((CELLS, PEERS), 1), 1.0, 0.0)
    every = dot(spread.astype(BF), want.astype(F32).astype(BF)).astype(I32)
    cell = iota((CELLS, 8), 0)
    mine = iota((CELLS, 8), 1) == (cell & 3) + first
    slot = jnp.sum(jnp.where(mine, every, 0), axis=1, keepdims=True)
    part = (iota((CELLS, 1), 0) >> 1) & 1
    held = jnp.where(slot < 0, -1, jnp.bitwise_xor(part, swap) * 16 + slot)
    return jnp.where(iota((CELLS, 32), 1) == held, 1.0, 0.0).astype(BF)


def answer_kernel(half_ref, want_ref, rows_ref, place_ref, out_ref, place_out_ref):
    place_out_ref[...] = place_ref[...]
    out_ref[...] = dot(picks(want_ref[...], half_ref[0], 0), rows_ref[...]).astype(BF).reshape(PEERS, 4, WIDTH)


def task_kernel(place_ref, rows_ref, tile_hbm, out_ref, tile_ref, sems):
    loads = [
        pltpu.make_async_copy(tile_hbm.at[pl.ds(k, n)], tile_ref.at[pl.ds(k, n)], sems.at[i])
        for i, (k, n) in enumerate(CHUNKS)
    ]
    for load in loads:
        load.start()
    cell = iota((CELLS, TASKS), 0)
    gather = jnp.where(cell == place_ref[0:1, :], 1.0, 0.0).astype(BF)
    scatter = jnp.where(cell == place_ref[1:2, :], 1.0, 0.0).astype(BF)
    operand = dot(gather, rows_ref[...].reshape(CELLS, WIDTH), 0).astype(BF)
    total = jnp.zeros((TASKS, WIDTH), F32)
    for load, (k, n) in zip(loads, CHUNKS):
        load.wait()
        total = total + dot(operand[:, k : k + n], tile_ref[k : k + n, :])
    out_ref[...] = dot(scatter, total.astype(BF)).astype(BF).reshape(PEERS, 4, WIDTH)


def collect_kernel(want_ref, rows_ref, out_ref):
    out_ref[...] = dot(picks(want_ref[...], 0, 4), rows_ref[...].reshape(CELLS, WIDTH), 0).astype(BF)


VM = pl.BlockSpec(memory_space=pltpu.VMEM)
SM = pl.BlockSpec(memory_space=pltpu.SMEM)
HB = pl.BlockSpec(memory_space=pl.ANY)


def call(kernel, ins, outs, *args, scratch=(), limit=None):
    shapes = tuple(jax.ShapeDtypeStruct(s, d) for s, d in outs)
    return pl.pallas_call(
        kernel,
        out_shape=shapes,
        in_specs=list(ins),
        out_specs=tuple(VM for _ in shapes),
        scratch_shapes=list(scratch),
        compiler_params=pltpu.CompilerParams(vmem_limit_bytes=limit),
    )(*args)


def return_pairs():
    pairs = []
    for a in range(2):
        for b in range(4):
            for k in range(2):
                for y in range(4):
                    pairs.append((((4 * a + b) * 2 + k) * 4 + y, ((4 * k + y) * 2 + a) * 4 + b))
    return pairs


def per_device(
    amplitudes, denominators, integrals, amp_owner, amp_slot, res_owner, res_slot, task_count
):
    half = (lax.axis_index("zh") // 4).astype(I32).reshape(1)
    other = lax.optimization_barrier(lax.ppermute(amplitudes, "core", ((0, 1), (1, 0))))
    pair = jnp.concatenate([amplitudes, other]).astype(BF)
    want, place = call(
        index_kernel,
        (SM, HB, HB, HB, HB),
        (((PEERS, 8), I32), ((8, TASKS), I32)),
        task_count,
        amp_owner.reshape(1, TASKS),
        amp_slot.reshape(1, TASKS),
        res_owner.reshape(1, TASKS),
        res_slot.reshape(1, TASKS),
        scratch=[pltpu.VMEM((1, TASKS), I32)] * 4 + [pltpu.SemaphoreType.DMA((4,))],
    )
    pair, want = lax.optimization_barrier((pair, want))
    held = lax.ppermute(pair, RING, [(d, s) for s, d in return_pairs()])
    wanted = lax.all_to_all(want.reshape(PEERS, 1, 8), BLOCK, 0, 0, tiled=True).reshape(PEERS, 8)
    found, place = call(
        answer_kernel,
        (SM, VM, VM, VM),
        (((PEERS, 4, WIDTH), BF), ((8, TASKS), I32)),
        half,
        wanted,
        held,
        place,
        limit=16 << 20,
    )
    fetched = lax.all_to_all(found, BLOCK, 0, 0, tiled=True)
    (sent,) = call(
        task_kernel,
        (VM, VM, HB),
        (((PEERS, 4, WIDTH), BF),),
        place,
        fetched,
        integrals,
        scratch=[pltpu.VMEM((WIDTH, WIDTH), BF), pltpu.SemaphoreType.DMA((len(CHUNKS),))],
        limit=50 << 20,
    )
    landed = lax.all_to_all(sent, BLOCK, 0, 0, tiled=True)
    (part,) = call(
        collect_kernel,
        (VM, VM),
        (((32, WIDTH), BF),),
        wanted,
        landed,
        limit=16 << 20,
    )
    back = lax.ppermute(part, RING, return_pairs())
    copies = jnp.broadcast_to(back.reshape(2, 1, 16, WIDTH), (2, 4, 16, WIDTH))
    every = lax.all_to_all(copies.reshape(8, 16, WIDTH), ("core", "rep"), 0, 0, tiled=True)
    residual = jnp.sum(every.astype(F32), axis=0)
    return residual, amplitudes + residual / denominators


def solution(mesh):
    fine = Mesh(mesh.devices.reshape(4, 8, 2, 2, 4), ("x", "zh", "zl", "core", "rep"))
    grid = ("x", "zh", "zl", "core")
    every = grid + ("rep",)
    return jax.shard_map(
        per_device,
        mesh=fine,
        in_specs=(
            P(grid, None),
            P(grid, None),
            P(every, None),
            P(every, None),
            P(every),
            P(every, None),
            P(every),
            P(every),
        ),
        out_specs=(P(grid, None), P(grid, None)),
        check_vma=False,
    )
```

```python
import jax
import jax.numpy as jnp
from jax import lax
from jax.experimental import pallas as pl
from jax.experimental.pallas import tpu as pltpu
from jax.sharding import Mesh, PartitionSpec as P

BF = jnp.bfloat16
F32 = jnp.float32
I32 = jnp.int32
TASKS = 128
PEERS = 64
CELLS = 256
WIDTH = 1440
CHUNKS = ((0, 384), (384, 384), (768, 384), (1152, 288))
BLOCK = ("core", "x", "zl", "rep")
RING = ("zh", "core", "rep")


def iota(shape, dim):
    return lax.broadcasted_iota(I32, shape, dim)


def dot(a, b, side=1):
    return lax.dot_general(a, b, (((side,), (0,)), ((), ())), preferred_element_type=F32)


def cells(owner, rank):
    core = owner & 1
    zl = (owner >> 1) & 1
    zh = (owner >> 2) & 7
    x = owner >> 5
    peer = (((zh >> 2) * 4 + x) * 2 + zl) * 4 + (zh & 3)
    return peer * 4 + core * 2 + rank


def index_kernel(
    count_ref, ao_hbm, as_hbm, ro_hbm, rs_hbm, want_ref, place_ref,
    ao_ref, as_ref, ro_ref, rs_ref, sems,
):
    moves = [
        pltpu.make_async_copy(src, dst, sems.at[i])
        for i, (src, dst) in enumerate(
            ((ao_hbm, ao_ref), (as_hbm, as_ref), (ro_hbm, ro_ref), (rs_hbm, rs_ref))
        )
    ]
    for move in moves:
        move.start()
    for move in moves:
        move.wait()
    square = (TASKS, TASKS)
    row, col = iota(square, 0), iota(square, 1)

    def to_col(vec):
        return jnp.sum(jnp.where(row == col, vec, 0), axis=1, keepdims=True)

    live_row = iota((1, TASKS), 1) < count_ref[0]
    total = jnp.zeros((PEERS, 8), F32)
    places = []
    for which, (o_ref, s_ref) in enumerate(((ao_ref, as_ref), (ro_ref, rs_ref))):
        owner_row = o_ref[...]
        same = to_col(owner_row) == owner_row
        rank = jnp.sum(jnp.where(same & (row < col), 1, 0), axis=0, keepdims=True)
        place = cells(owner_row, rank)
        mine = (iota((8, TASKS), 0) == (place & 3) + 4 * which) & live_row
        value = jnp.where(mine, s_ref[...] + 1, 0)
        peer = jnp.where(iota((PEERS, TASKS), 0) == (place >> 2), 1.0, 0.0)
        total = total + lax.dot_general(
            peer.astype(BF),
            value.astype(F32).astype(BF),
            (((1,), (1,)), ((), ())),
            preferred_element_type=F32,
        )
        places.append(jnp.where(live_row, place, -1))
    want_ref[...] = total.astype(I32) - 1
    which = iota((8, TASKS), 0)
    place_ref[...] = jnp.where(which == 0, places[0], places[1])


def picks(want, swap, first):
    spread = jnp.where(iota((CELLS, PEERS), 0) >> 2 == iota((CELLS, PEERS), 1), 1.0, 0.0)
    every = dot(spread.astype(BF), want.astype(F32).astype(BF)).astype(I32)
    cell = iota((CELLS, 8), 0)
    mine = iota((CELLS, 8), 1) == (cell & 3) + first
    slot = jnp.sum(jnp.where(mine, every, 0), axis=1, keepdims=True)
    part = (iota((CELLS, 1), 0) >> 1) & 1
    held = jnp.where(slot < 0, -1, jnp.bitwise_xor(part, swap) * 16 + slot)
    return jnp.where(iota((CELLS, 32), 1) == held, 1.0, 0.0).astype(BF)


def answer_kernel(half_ref, want_ref, rows_ref, place_ref, out_ref, place_out_ref):
    place_out_ref[...] = place_ref[...]
    out_ref[...] = dot(picks(want_ref[...], half_ref[0], 0), rows_ref[...]).astype(BF).reshape(PEERS, 4, WIDTH)


def task_kernel(place_ref, rows_ref, tile_hbm, out_ref, tile_ref, sems):
    loads = [
        pltpu.make_async_copy(tile_hbm.at[pl.ds(k, n)], tile_ref.at[pl.ds(k, n)], sems.at[i])
        for i, (k, n) in enumerate(CHUNKS)
    ]
    for load in loads:
        load.start()
    cell = iota((CELLS, TASKS), 0)
    gather = jnp.where(cell == place_ref[0:1, :], 1.0, 0.0).astype(BF)
    scatter = jnp.where(cell == place_ref[1:2, :], 1.0, 0.0).astype(BF)
    operand = dot(gather, rows_ref[...].reshape(CELLS, WIDTH), 0).astype(BF)
    total = jnp.zeros((TASKS, WIDTH), F32)
    for load, (k, n) in zip(loads, CHUNKS):
        load.wait()
        total = total + dot(operand[:, k : k + n], tile_ref[k : k + n, :])
    out_ref[...] = dot(scatter, total.astype(BF)).astype(BF).reshape(PEERS, 4, WIDTH)


def collect_kernel(want_ref, rows_ref, out_ref):
    out_ref[...] = dot(picks(want_ref[...], 0, 4), rows_ref[...].reshape(CELLS, WIDTH), 0).astype(BF)


VM = pl.BlockSpec(memory_space=pltpu.VMEM)
SM = pl.BlockSpec(memory_space=pltpu.SMEM)
HB = pl.BlockSpec(memory_space=pl.ANY)


def call(kernel, ins, outs, *args, scratch=(), limit=None):
    shapes = tuple(jax.ShapeDtypeStruct(s, d) for s, d in outs)
    return pl.pallas_call(
        kernel,
        out_shape=shapes,
        in_specs=list(ins),
        out_specs=tuple(VM for _ in shapes),
        scratch_shapes=list(scratch),
        compiler_params=pltpu.CompilerParams(vmem_limit_bytes=limit),
    )(*args)


LANDING = ((2, 0), (3, 1), (1, 1), (0, 1), (0, 0), (1, 0), (3, 0), (2, 1))


def return_pairs():
    pairs = []
    for zh in range(8):
        for core in range(2):
            for rep in range(4):
                home = 4 * core + rep
                step, to_core = LANDING[(zh - home) % 8]
                target = (home * 2 + to_core) * 4 + (rep + step) % 4
                pairs.append(((zh * 2 + core) * 4 + rep, target))
    return pairs


def spread_pairs():
    pairs = []
    for a in range(2):
        for b in range(4):
            for k in range(2):
                for y in range(4):
                    pairs.append((((4 * a + b) * 2 + k) * 4 + y, ((4 * k + y) * 2 + a) * 4 + (b ^ y)))
    return pairs


def per_device(
    amplitudes, denominators, integrals, amp_owner, amp_slot, res_owner, res_slot, task_count
):
    half = (lax.axis_index("zh") // 4).astype(I32).reshape(1)
    other = lax.optimization_barrier(lax.ppermute(amplitudes, "core", ((0, 1), (1, 0))))
    pair = jnp.concatenate([amplitudes, other]).astype(BF)
    want, place = call(
        index_kernel,
        (SM, HB, HB, HB, HB),
        (((PEERS, 8), I32), ((8, TASKS), I32)),
        task_count,
        amp_owner.reshape(1, TASKS),
        amp_slot.reshape(1, TASKS),
        res_owner.reshape(1, TASKS),
        res_slot.reshape(1, TASKS),
        scratch=[pltpu.VMEM((1, TASKS), I32)] * 4 + [pltpu.SemaphoreType.DMA((4,))],
    )
    pair, want = lax.optimization_barrier((pair, want))
    held = lax.ppermute(pair, RING, [(d, s) for s, d in spread_pairs()])
    wanted = lax.all_to_all(want.reshape(PEERS, 1, 8), BLOCK, 0, 0, tiled=True).reshape(PEERS, 8)
    found, place = call(
        answer_kernel,
        (SM, VM, VM, VM),
        (((PEERS, 4, WIDTH), BF), ((8, TASKS), I32)),
        half,
        wanted,
        held,
        place,
        limit=16 << 20,
    )
    fetched = lax.all_to_all(found, BLOCK, 0, 0, tiled=True)
    (sent,) = call(
        task_kernel,
        (VM, VM, HB),
        (((PEERS, 4, WIDTH), BF),),
        place,
        fetched,
        integrals,
        scratch=[pltpu.VMEM((WIDTH, WIDTH), BF), pltpu.SemaphoreType.DMA((len(CHUNKS),))],
        limit=50 << 20,
    )
    landed = lax.all_to_all(sent, BLOCK, 0, 0, tiled=True)
    (part,) = call(
        collect_kernel,
        (VM, VM),
        (((32, WIDTH), BF),),
        wanted,
        landed,
        limit=16 << 20,
    )
    back = lax.ppermute(part, RING, return_pairs())
    copies = jnp.broadcast_to(back.reshape(2, 1, 16, WIDTH), (2, 4, 16, WIDTH))
    every = lax.all_to_all(copies.reshape(8, 16, WIDTH), ("core", "rep"), 0, 0, tiled=True)
    residual = jnp.sum(every.astype(F32), axis=0)
    return residual, amplitudes + residual / denominators


def solution(mesh):
    fine = Mesh(mesh.devices.reshape(4, 8, 2, 2, 4), ("x", "zh", "zl", "core", "rep"))
    grid = ("x", "zh", "zl", "core")
    every = grid + ("rep",)
    return jax.shard_map(
        per_device,
        mesh=fine,
        in_specs=(
            P(grid, None),
            P(grid, None),
            P(every, None),
            P(every, None),
            P(every),
            P(every, None),
            P(every),
            P(every),
        ),
        out_specs=(P(grid, None), P(grid, None)),
        check_vma=False,
    )
```

```python
import jax
import jax.numpy as jnp
from jax import lax
from jax.experimental import pallas as pl
from jax.experimental.pallas import tpu as pltpu
from jax.sharding import Mesh, PartitionSpec as P

BF = jnp.bfloat16
F32 = jnp.float32
I32 = jnp.int32
TASKS = 128
PEERS = 64
CELLS = 256
WIDTH = 1440
CHUNKS = ((0, 384), (384, 384), (768, 384), (1152, 288))
BLOCK = ("core", "x", "zl", "rep")
RING = ("zh", "core", "rep")


def iota(shape, dim):
    return lax.broadcasted_iota(I32, shape, dim)


def dot(a, b, side=1):
    return lax.dot_general(a, b, (((side,), (0,)), ((), ())), preferred_element_type=F32)


def cells(owner, rank):
    core = owner & 1
    zl = (owner >> 1) & 1
    zh = (owner >> 2) & 7
    x = owner >> 5
    peer = (((zh >> 2) * 4 + x) * 2 + zl) * 4 + (zh & 3)
    return peer * 4 + core * 2 + rank


def index_kernel(
    count_ref, ao_hbm, as_hbm, ro_hbm, rs_hbm, want_ref, place_ref,
    ao_ref, as_ref, ro_ref, rs_ref, sems,
):
    moves = [
        pltpu.make_async_copy(src, dst, sems.at[i])
        for i, (src, dst) in enumerate(
            ((ao_hbm, ao_ref), (as_hbm, as_ref), (ro_hbm, ro_ref), (rs_hbm, rs_ref))
        )
    ]
    for move in moves:
        move.start()
    for move in moves:
        move.wait()
    square = (TASKS, TASKS)
    row, col = iota(square, 0), iota(square, 1)

    def to_col(vec):
        return jnp.sum(jnp.where(row == col, vec, 0), axis=1, keepdims=True)

    live_row = iota((1, TASKS), 1) < count_ref[0]
    total = jnp.zeros((PEERS, 8), F32)
    places = []
    for which, (o_ref, s_ref) in enumerate(((ao_ref, as_ref), (ro_ref, rs_ref))):
        owner_row = o_ref[...]
        same = to_col(owner_row) == owner_row
        rank = jnp.sum(jnp.where(same & (row < col), 1, 0), axis=0, keepdims=True)
        place = cells(owner_row, rank)
        mine = (iota((8, TASKS), 0) == (place & 3) + 4 * which) & live_row
        value = jnp.where(mine, s_ref[...] + 1, 0)
        peer = jnp.where(iota((PEERS, TASKS), 0) == (place >> 2), 1.0, 0.0)
        total = total + lax.dot_general(
            peer.astype(BF),
            value.astype(F32).astype(BF),
            (((1,), (1,)), ((), ())),
            preferred_element_type=F32,
        )
        places.append(jnp.where(live_row, place, -1))
    want_ref[...] = total.astype(I32) - 1
    which = iota((8, TASKS), 0)
    place_ref[...] = jnp.where(which == 0, places[0], places[1])


def picks(want, swap, first):
    spread = jnp.where(iota((CELLS, PEERS), 0) >> 2 == iota((CELLS, PEERS), 1), 1.0, 0.0)
    every = dot(spread.astype(BF), want.astype(F32).astype(BF)).astype(I32)
    cell = iota((CELLS, 8), 0)
    mine = iota((CELLS, 8), 1) == (cell & 3) + first
    slot = jnp.sum(jnp.where(mine, every, 0), axis=1, keepdims=True)
    part = (iota((CELLS, 1), 0) >> 1) & 1
    held = jnp.where(slot < 0, -1, jnp.bitwise_xor(part, swap) * 16 + slot)
    return jnp.where(iota((CELLS, 32), 1) == held, 1.0, 0.0).astype(BF)


def answer_kernel(half_ref, want_ref, rows_ref, place_ref, out_ref, place_out_ref):
    place_out_ref[...] = place_ref[...]
    out_ref[...] = dot(picks(want_ref[...], half_ref[0], 0), rows_ref[...]).astype(BF).reshape(PEERS, 4, WIDTH)


def task_kernel(place_ref, rows_ref, tile_hbm, out_ref, tile_ref, sems):
    loads = [
        pltpu.make_async_copy(tile_hbm.at[pl.ds(k, n)], tile_ref.at[pl.ds(k, n)], sems.at[i])
        for i, (k, n) in enumerate(CHUNKS)
    ]
    for load in loads:
        load.start()
    cell = iota((CELLS, TASKS), 0)
    gather = jnp.where(cell == place_ref[0:1, :], 1.0, 0.0).astype(BF)
    scatter = jnp.where(cell == place_ref[1:2, :], 1.0, 0.0).astype(BF)
    operand = dot(gather, rows_ref[...].reshape(CELLS, WIDTH), 0).astype(BF)
    total = jnp.zeros((TASKS, WIDTH), F32)
    for load, (k, n) in zip(loads, CHUNKS):
        load.wait()
        total = total + dot(operand[:, k : k + n], tile_ref[k : k + n, :])
    out_ref[...] = dot(scatter, total.astype(BF)).astype(BF).reshape(PEERS, 4, WIDTH)


def collect_kernel(want_ref, rows_ref, out_ref):
    out_ref[...] = dot(picks(want_ref[...], 0, 4), rows_ref[...].reshape(CELLS, WIDTH), 0).astype(BF)


VM = pl.BlockSpec(memory_space=pltpu.VMEM)
SM = pl.BlockSpec(memory_space=pltpu.SMEM)
HB = pl.BlockSpec(memory_space=pl.ANY)


def call(kernel, ins, outs, *args, scratch=(), limit=None):
    shapes = tuple(
        pltpu.VMEM(s, d) if s == (8, TASKS) else jax.ShapeDtypeStruct(s, d) for s, d in outs
    )
    return pl.pallas_call(
        kernel,
        out_shape=shapes,
        in_specs=list(ins),
        out_specs=tuple(VM for _ in shapes),
        scratch_shapes=list(scratch),
        compiler_params=pltpu.CompilerParams(vmem_limit_bytes=limit),
    )(*args)


LANDING = ((2, 0), (3, 1), (1, 1), (0, 1), (0, 0), (1, 0), (3, 0), (2, 1))


def return_pairs():
    pairs = []
    for zh in range(8):
        for core in range(2):
            for rep in range(4):
                home = 4 * core + rep
                step, to_core = LANDING[(zh - home) % 8]
                target = (home * 2 + to_core) * 4 + (rep + step) % 4
                pairs.append(((zh * 2 + core) * 4 + rep, target))
    return pairs


def spread_pairs():
    pairs = []
    for a in range(2):
        for b in range(4):
            for k in range(2):
                for y in range(4):
                    pairs.append((((4 * a + b) * 2 + k) * 4 + y, ((4 * k + y) * 2 + a) * 4 + (b ^ y)))
    return pairs


def per_device(
    amplitudes, denominators, integrals, amp_owner, amp_slot, res_owner, res_slot, task_count
):
    half = (lax.axis_index("zh") // 4).astype(I32).reshape(1)
    other = lax.optimization_barrier(lax.ppermute(amplitudes, "core", ((0, 1), (1, 0))))
    pair = jnp.concatenate([amplitudes, other]).astype(BF)
    want, place = call(
        index_kernel,
        (SM, HB, HB, HB, HB),
        (((PEERS, 8), I32), ((8, TASKS), I32)),
        task_count,
        amp_owner.reshape(1, TASKS),
        amp_slot.reshape(1, TASKS),
        res_owner.reshape(1, TASKS),
        res_slot.reshape(1, TASKS),
        scratch=[pltpu.VMEM((1, TASKS), I32)] * 4 + [pltpu.SemaphoreType.DMA((4,))],
    )
    pair, want = lax.optimization_barrier((pair, want))
    held = lax.ppermute(pair, RING, [(d, s) for s, d in spread_pairs()])
    wanted = lax.all_to_all(want.reshape(PEERS, 1, 8), BLOCK, 0, 0, tiled=True).reshape(PEERS, 8)
    found, place = call(
        answer_kernel,
        (SM, VM, VM, VM),
        (((PEERS, 4, WIDTH), BF), ((8, TASKS), I32)),
        half,
        wanted,
        held,
        place,
        limit=16 << 20,
    )
    fetched = lax.all_to_all(found, BLOCK, 0, 0, tiled=True)
    (sent,) = call(
        task_kernel,
        (VM, VM, HB),
        (((PEERS, 4, WIDTH), BF),),
        place,
        fetched,
        integrals,
        scratch=[pltpu.VMEM((WIDTH, WIDTH), BF), pltpu.SemaphoreType.DMA((len(CHUNKS),))],
        limit=50 << 20,
    )
    landed = lax.all_to_all(sent, BLOCK, 0, 0, tiled=True)
    (part,) = call(
        collect_kernel,
        (VM, VM),
        (((32, WIDTH), BF),),
        wanted,
        landed,
        limit=16 << 20,
    )
    back = lax.ppermute(part, RING, return_pairs())
    copies = jnp.broadcast_to(back.reshape(2, 1, 16, WIDTH), (2, 4, 16, WIDTH))
    every = lax.all_to_all(copies.reshape(8, 16, WIDTH), ("core", "rep"), 0, 0, tiled=True)
    residual = jnp.sum(every.astype(F32), axis=0)
    return residual, amplitudes + residual / denominators


def solution(mesh):
    fine = Mesh(mesh.devices.reshape(4, 8, 2, 2, 4), ("x", "zh", "zl", "core", "rep"))
    grid = ("x", "zh", "zl", "core")
    every = grid + ("rep",)
    return jax.shard_map(
        per_device,
        mesh=fine,
        in_specs=(
            P(grid, None),
            P(grid, None),
            P(every, None),
            P(every, None),
            P(every),
            P(every, None),
            P(every),
            P(every),
        ),
        out_specs=(P(grid, None), P(grid, None)),
        check_vma=False,
    )
```
